32 devices in a mesh: dom: 8 (over z, y), feat: 4 (over x, core).
Axes of the slice: x: 2, y: 2, z: 4, core: 2. Of those that a mesh axis runs over, the one named last changes fastest.
Arguments:
- nodes: bfloat16 [8192, 512], P('dom'), may hold values from -36 to 36
- walk_state: bfloat16 [8192, 256], P('dom', 'feat'), may hold values from -6 to 6
- walk_values: bfloat16 [64, 8, 128, 128], P('dom'), may hold values from -0.1875 to 0.1875
- walk_cols: int32 [64, 8], P('dom'), may hold values from 0 to 63, as said below
- walk_count: int32 [64], P('dom'), may hold values from 1 to 8
- attn_cols: int32 [64, 8], P('dom'), may hold values from 0 to 63, as said below
- attn_count: int32 [64], P('dom'), may hold values from 1 to 8
- w_query: bfloat16 [512, 512], P(None, 'feat'), may hold values from -0.25 to 0.25
- w_key: bfloat16 [512, 512], P(None, 'feat'), may hold values from -0.25 to 0.25
- w_value: bfloat16 [512, 512], P(None, 'feat'), may hold values from -0.25 to 0.25
- bias_query: bfloat16 [2, 256, 512], P(None, 'feat'), may hold values from -0.25 to 0.25
- bias_key: bfloat16 [2, 256, 512], P(None, 'feat'), may hold values from -0.25 to 0.25
- w_out: bfloat16 [512, 512], P('feat'), may hold values from -0.75 to 0.75
Outputs:
- new_nodes: bfloat16 [8192, 512], P('dom', 'feat')
- walk_next: bfloat16 [8192, 256], P('dom', 'feat')
The draws below stay inside these ranges and needn't reach their ends.
Inputs may be any that keep to these rules, and one draw needn't show every extreme that they name: `walk_cols`: A column block of row block b lies in partitions b // 8 - 2 to b // 8 + 2, taken cyclically over the 8 partitions; slot 0 is b itself. `attn_cols`: A key block of row block b lies in partitions b // 8 - 2 to b // 8 + 2, taken cyclically over the 8 partitions; slot 0 is b itself.
All inputs are finite; a program needn't handle non-finite values.
Results may differ from the reference program's by a relative error of at most 0.015.
The reference program's roundings to bfloat16 on the way count: a program that leaves them out, or rounds other values in their place, can miss the bound.
Values may be sent and summed in bfloat16 or wider, within the bound.
A program may use at most 64 MiB of HBM per device.

```python
import jax
import jax.numpy as jnp
from jax import lax

D = 512
H = 8
HD = 64
K = 256
BR = 64
BS = 128
NBD = 8
EMAX = 8
EA = 8
R = 2
NB = 64
N = 8192
N_FEAT = 4


def draw_block_links(key, slot_total):
    partitions = NB // NBD
    key_step, key_inner = jax.random.split(key)
    block_ids = jnp.arange(NB, dtype=jnp.int32)[:, None]
    step_offset = jax.random.randint(key_step, (NB, slot_total), -R, R + 1)
    inner_block = jax.random.randint(key_inner, (NB, slot_total), 0, NBD)
    home_part = block_ids // NBD
    linked = jnp.mod(home_part + step_offset, partitions) * NBD + inner_block
    linked = jnp.where(jnp.arange(slot_total)[None, :] == 0, block_ids, linked)
    return linked.astype(jnp.int32)


def draw_slot_counts(key, most_slots):
    key_count, key_pick = jax.random.split(key)
    counts = jax.random.randint(key_count, (NB,), 1, most_slots + 1)
    chosen = jax.random.randint(key_pick, (), 0, NB)
    counts = jnp.where(jnp.arange(NB) == chosen, most_slots, counts)
    return counts.astype(jnp.int32)


def draw_walk_cols(key, part):
    return draw_block_links(jax.random.fold_in(key, 11), EMAX)


def draw_attn_cols(key, part):
    return draw_block_links(jax.random.fold_in(key, 23), EA)


def draw_walk_count(key, part):
    return draw_slot_counts(jax.random.fold_in(key, 37), EMAX)


def draw_attn_count(key, part):
    return draw_slot_counts(jax.random.fold_in(key, 41), EA)


def draw_nodes(key, part):
    key_base = jax.random.fold_in(jax.random.fold_in(key, 53), 0)
    base_values = jnp.clip(jax.random.normal(key_base, (N, D), jnp.float32), -6.0, 6.0)
    return base_values.astype(jnp.bfloat16)


def block_levels(rng, extent, cuts, smallest, largest):
    def one(dim, shards_of):
        draws = jax.random.uniform(jax.random.fold_in(jax.random.fold_in(rng, 6), dim), (shards_of,), jnp.float32, smallest / len(cuts), largest / len(cuts))
        return jnp.repeat(jnp.exp(draws), extent[dim] // shards_of).reshape((-1,) + (1,) * (len(extent) - dim - 1))

    factor_of = one(*cuts[0])
    for cut in cuts[1:]:
        factor_of = factor_of * one(*cut)
    return factor_of


def scatter_about(key, extent, width, limit, cuts=(), kind=jnp.bfloat16):
    gain = block_levels(key, extent, cuts, -0.22, 0.18) if cuts else 1.0
    array = jax.random.normal(key, extent, jnp.float32) * width * gain
    return jnp.minimum(jnp.maximum(array, -limit), limit).astype(kind)


def setup_inputs(seed: int = 0) -> dict:
    key_list = jax.random.split(jax.random.key(seed), 14)
    return {
        "nodes": draw_nodes(jax.random.fold_in(key_list[13], 71), 0),
        "walk_state": scatter_about(key_list[1], (N, K), 1.0, 6.0, ((0, 8), (1, 4))),
        "walk_values": scatter_about(key_list[2], (NB, EMAX, BS, BS), (EMAX * BS) ** -0.5, 0.1875, ((0, 8),)),
        "walk_cols": draw_walk_cols(jax.random.fold_in(key_list[13], 71), 0),
        "walk_count": draw_walk_count(jax.random.fold_in(key_list[13], 71), 0),
        "attn_cols": draw_attn_cols(jax.random.fold_in(key_list[13], 71), 0),
        "attn_count": draw_attn_count(jax.random.fold_in(key_list[13], 71), 0),
        "w_query": scatter_about(key_list[7], (D, D), D ** -0.5, 0.25, ((1, 4),)),
        "w_key": scatter_about(key_list[8], (D, D), D ** -0.5, 0.25, ((1, 4),)),
        "w_value": scatter_about(key_list[9], (D, D), D ** -0.5, 0.25, ((1, 4),)),
        "bias_query": scatter_about(key_list[10], (2, K, H * BR), (2 * K) ** -0.5, 0.25, ((1, 4),)),
        "bias_key": scatter_about(key_list[11], (2, K, H * BR), (2 * K) ** -0.5, 0.25, ((1, 4),)),
        "w_out": scatter_about(key_list[12], (D, D), (D // 8) ** -0.5, 0.75, ((0, 4),)),
    }


def propagate(state, walk_values, walk_cols, walk_count):
    state_blocks = state.reshape(NB, BS, K)
    live_slot = jnp.arange(EMAX)[None, :] < walk_count[:, None]

    def walk_block(inputs):
        block_vals, block_ids, live_row = inputs
        block_vals = jnp.where(live_row[:, None, None], block_vals, jnp.zeros_like(block_vals))
        near_blocks = state_blocks[block_ids]
        return jnp.einsum('eij,ejk->ik', block_vals.astype(jnp.float32), near_blocks.astype(jnp.float32))

    result = lax.map(walk_block, (walk_values, walk_cols, live_slot))
    return result.reshape(N, K).astype(jnp.bfloat16)


def bias_project(feats, weight):
    group_width = K // N_FEAT
    totals = jnp.zeros((N, H * BR), jnp.float32)
    for group_id in range(N_FEAT):
        lower = group_id * group_width
        partial_sum = jnp.einsum('nsk,skc->nc', feats[:, :, lower:lower + group_width].astype(jnp.float32), weight[:, lower:lower + group_width].astype(jnp.float32))
        totals = totals + partial_sum.astype(jnp.bfloat16).astype(jnp.float32)
    return totals.astype(jnp.bfloat16)


def reference(nodes, walk_state, walk_values, walk_cols, walk_count, attn_cols, attn_count, w_query, w_key, w_value, bias_query, bias_key, w_out):
    walk_one = propagate(walk_state, walk_values, walk_cols, walk_count)
    walk_next = propagate(walk_one, walk_values, walk_cols, walk_count)
    feats = jnp.stack([walk_one, walk_next], axis=1)
    bias_q = bias_project(feats, bias_query)
    bias_k = bias_project(feats, bias_key)
    queries = jnp.dot(nodes, w_query, preferred_element_type=jnp.float32).astype(jnp.bfloat16)
    keys = jnp.dot(nodes, w_key, preferred_element_type=jnp.float32).astype(jnp.bfloat16)
    vals = jnp.dot(nodes, w_value, preferred_element_type=jnp.float32).astype(jnp.bfloat16)
    query_blocks = queries.reshape(NB, BS, H, HD)
    key_blocks = keys.reshape(NB, BS, H, HD)
    value_blocks = vals.reshape(NB, BS, H, HD)
    bias_qblocks = bias_q.reshape(NB, BS, H, BR)
    bias_kblocks = bias_k.reshape(NB, BS, H, BR)

    def attend(inputs):
        query_rows, bias_rows, block_ids, slot_count = inputs
        key_near = key_blocks[block_ids].astype(jnp.float32)
        value_near = value_blocks[block_ids].astype(jnp.float32)
        bias_near = bias_kblocks[block_ids].astype(jnp.float32)
        scores = jnp.einsum('ihd,ejhd->hiej', query_rows.astype(jnp.float32), key_near) * (HD ** -0.5)
        scores = scores + jnp.einsum('ihr,ejhr->hiej', bias_rows.astype(jnp.float32), bias_near) * (BR ** -0.5)
        live_slot = (jnp.arange(EA) < slot_count)[None, None, :, None]
        scores = jnp.where(live_slot, scores, -1e30)
        top_score = jnp.max(scores, axis=(2, 3), keepdims=True)
        expo = jnp.exp(scores - top_score)
        weights = (expo / jnp.sum(expo, axis=(2, 3), keepdims=True)).astype(jnp.bfloat16)
        return jnp.einsum('hiej,ejhd->ihd', weights.astype(jnp.float32), value_near).astype(jnp.bfloat16)

    attended = lax.map(attend, (query_blocks, bias_qblocks, attn_cols, attn_count)).reshape(N, D)
    group_width = D // N_FEAT
    totals = jnp.zeros((N, D), jnp.float32)
    for group_id in range(N_FEAT):
        lower = group_id * group_width
        partial_sum = jnp.dot(attended[:, lower:lower + group_width], w_out[lower:lower + group_width], preferred_element_type=jnp.float32)
        totals = totals + partial_sum.astype(jnp.bfloat16).astype(jnp.float32)
    new_nodes = totals.astype(jnp.bfloat16)
    return (new_nodes, walk_next)
```

```python
import functools

import jax
import jax.numpy as jnp
from jax import lax
from jax.experimental import pallas as pl
from jax.experimental.pallas import tpu as pltpu
from jax.sharding import PartitionSpec as P

HD = 64
BS = 128
R = 2
MESH = pl.DeviceIdType.MESH
OFFSETS = tuple(o for o in range(-R, R + 1) if o != 0)
LOG2E = 1.4426950408889634


def dot(left, right):
    return jnp.dot(left, right, preferred_element_type=jnp.float32)


def dot_t(left, right):
    return lax.dot_general(
        left, right, (((1,), (1,)), ((), ())), preferred_element_type=jnp.float32
    )


def kernel(
    sizes,
    walk_cols,
    walk_count,
    attn_cols,
    attn_count,
    nodes,
    walk_state,
    walk_values,
    w_query,
    w_key,
    w_value,
    bias_query,
    bias_key,
    w_out,
    new_nodes,
    walk_next,
    win0,
    win1,
    kv,
    bk,
    f1,
    f2,
    bw,
    wbd,
    queries,
    biasq,
    stage,
    landed,
    state_send,
    state_recv,
    one_send,
    one_recv,
    kv_send,
    kv_recv,
    bk_send,
    bk_recv,
    f1_send,
    f1_recv,
    f2_send,
    f2_recv,
    bw_send,
    bw_recv,
    out_send,
    out_recv,
):
    n_dom, n_feat, blocks, walk_slots, attn_slots = sizes
    half = blocks // 2
    window_blocks = (2 * R + 1) * blocks
    total = n_dom * blocks
    me_dom = lax.axis_index("dom")
    me_feat = lax.axis_index("feat")
    first = (me_dom - R) * blocks
    near = [lax.rem(me_dom + o + n_dom, n_dom) for o in OFFSETS]
    peers = [lax.rem(me_feat + d, n_feat) for d in range(1, n_feat)]
    lane = lax.broadcasted_iota(jnp.int32, (1, BS), 1)
    lane_half = lax.div(lane, HD)

    def place(block_id):
        pos = lax.rem(block_id - first + total, total)
        return jnp.minimum(pos, window_blocks - 1)

    def to_dom(buffer, per, send, recv):
        copies = []
        for i, o in enumerate(OFFSETS):
            copies.append(
                pltpu.make_async_remote_copy(
                    src_ref=buffer.at[pl.ds(R * per, per)],
                    dst_ref=buffer.at[pl.ds((R - o) * per, per)],
                    send_sem=send.at[i],
                    recv_sem=recv.at[i],
                    device_id={"dom": near[i]},
                    device_id_type=MESH,
                )
            )
        return copies

    def to_feat(buffer, per, send, recv):
        copies = []
        mine = pl.ds(me_feat * per, per)
        for i, peer in enumerate(peers):
            copies.append(
                pltpu.make_async_remote_copy(
                    src_ref=buffer.at[mine],
                    dst_ref=buffer.at[mine],
                    send_sem=send.at[i],
                    recv_sem=recv.at[i],
                    device_id={"feat": peer},
                    device_id_type=MESH,
                )
            )
        return copies

    def start(copies):
        for copy in copies:
            copy.start()

    def wait_recv(copies):
        for copy in copies:
            copy.wait_recv()

    win0[pl.ds(R * half, half)] = jnp.concatenate(
        [walk_state[: half * BS, :], walk_state[half * BS :, :]], axis=1
    ).reshape(half, BS, BS)

    barrier = pltpu.get_barrier_semaphore()
    for device in near:
        pl.semaphore_signal(barrier, inc=1, device_id={"dom": device}, device_id_type=MESH)
    for device in peers:
        pl.semaphore_signal(barrier, inc=1, device_id={"feat": device}, device_id_type=MESH)
    pl.semaphore_wait(barrier, len(near) + len(peers))

    state_copies = to_dom(win0, half, state_send, state_recv)
    start(state_copies)
    bw_copies = []
    for t, weight in enumerate((bias_query, bias_key)):
        for i, peer in enumerate(peers):
            bw_copies.append(
                pltpu.make_async_remote_copy(
                    src_ref=weight.at[:, :, pl.ds(pl.multiple_of(peer * BS, BS), BS)],
                    dst_ref=bw.at[me_feat, t],
                    send_sem=bw_send.at[t, i],
                    recv_sem=bw_recv.at[t, i],
                    device_id={"feat": peer},
                    device_id_type=MESH,
                )
            )
    start(bw_copies)

    w_all = jnp.concatenate([w_query[...], w_key[...], w_value[...]], axis=1)

    def project(i, carry):
        rows = nodes[pl.ds(pl.multiple_of(i * 2 * BS, 2 * BS), 2 * BS), :]
        product = dot(rows, w_all).astype(jnp.bfloat16)
        queries[pl.ds(2 * i, 2)] = product[:, :BS].reshape(2, BS, BS)
        kv[pl.ds(2 * R * blocks + 2 * i, 2)] = product[:, BS : 2 * BS].reshape(2, BS, BS)
        kv[pl.ds((2 * R + 1) * blocks + 2 * i, 2)] = product[:, 2 * BS :].reshape(2, BS, BS)
        return carry

    lax.fori_loop(0, blocks // 2, project, 0)

    def walk_rows(window, b):
        count = walk_count[b]
        parts = []
        for e in range(walk_slots):
            pos = place(walk_cols[b, e])
            part = lax.div(pos, blocks)
            block = lax.rem(pos, blocks)
            side = jnp.where(e < count, lax.div(block, half), 2)
            keep = jnp.where(lane_half == side, 1.0, 0.0).astype(jnp.bfloat16)
            parts.append(window[part * half + lax.rem(block, half)] * keep)
        left = jnp.concatenate([walk_values[b, e] for e in range(walk_slots)], axis=1)
        both = dot(left, jnp.concatenate(parts, axis=0))
        return both + pltpu.roll(both, HD, 1)

    def walk_pair(window, j):
        low = walk_rows(window, j)
        high = walk_rows(window, j + half)
        return jnp.where(lane < HD, low, high).astype(jnp.bfloat16)

    wait_recv(state_copies)

    def step_one(j, carry):
        pair = walk_pair(win0, j)
        win1[R * half + j] = pair
        f1[me_feat * half + j] = pair
        return carry

    lax.fori_loop(0, half, step_one, 0)
    one_copies = to_dom(win1, half, one_send, one_recv)
    start(one_copies)
    f1_copies = to_feat(f1, half, f1_send, f1_recv)
    start(f1_copies)
    kv_copies = to_dom(kv, 2 * blocks, kv_send, kv_recv)
    start(kv_copies)

    own = pl.ds(pl.multiple_of(me_feat * BS, BS), BS)
    bw[me_feat, 0] = bias_query[:, :, own]
    bw[me_feat, 1] = bias_key[:, :, own]
    wait_recv(bw_copies)
    zero = jnp.zeros((HD, BS), jnp.bfloat16)

    def spread(g, carry):
        for t in range(2):
            for s in range(2):
                weight = bw[g, t, s]
                wbd[g, t, pl.ds(s * BS, HD), :] = jnp.concatenate([weight, zero], axis=1)
                wbd[g, t, pl.ds(s * BS + HD, HD), :] = jnp.concatenate([zero, weight], axis=1)
        return carry

    lax.fori_loop(0, n_feat, spread, 0)

    wait_recv(one_copies)

    def step_two(j, carry):
        pair = walk_pair(win1, j)
        f2[me_feat * half + j] = pair
        walk_next[pl.ds(pl.multiple_of(j * BS, BS), BS), :] = pair[:, :HD]
        walk_next[pl.ds(pl.multiple_of((j + half) * BS, BS), BS), :] = pair[:, HD:]
        return carry

    lax.fori_loop(0, half, step_two, 0)
    f2_copies = to_feat(f2, half, f2_send, f2_recv)
    start(f2_copies)
    wait_recv(f1_copies)
    wait_recv(f2_copies)

    def bias(j, carry):
        sums = [None, None]
        for g in range(n_feat):
            feats = jnp.concatenate([f1[g * half + j], f2[g * half + j]], axis=1)
            for t in range(2):
                term = dot(feats, wbd[g, t]).astype(jnp.bfloat16).astype(jnp.float32)
                sums[t] = term if sums[t] is None else sums[t] + term
        bias_q, bias_k = sums[0].astype(jnp.bfloat16), sums[1].astype(jnp.bfloat16)
        biasq[j] = bias_q[:, :BS]
        biasq[j + half] = bias_q[:, BS:]
        bk[R * blocks + j] = bias_k[:, :BS]
        bk[R * blocks + j + half] = bias_k[:, BS:]
        return carry

    lax.fori_loop(0, half, bias, 0)
    bk_copies = to_dom(bk, blocks, bk_send, bk_recv)
    start(bk_copies)
    wait_recv(kv_copies)
    wait_recv(bk_copies)

    def out_copies(b):
        return [
            pltpu.make_async_remote_copy(
                src_ref=stage.at[b * n_feat + peer],
                dst_ref=landed.at[b * (n_feat - 1) + i],
                send_sem=out_send.at[b, i],
                recv_sem=out_recv.at[b, i],
                device_id={"feat": peer},
                device_id_type=MESH,
            )
            for i, peer in enumerate(peers)
        ]

    first_head = jnp.where(lane < HD, 1.0, 0.0).astype(jnp.bfloat16)
    second_head = jnp.where(lane < HD, 0.0, 1.0).astype(jnp.bfloat16)

    def attend(b, carry):
        count = attn_count[b]
        query, bias_q = queries[b], biasq[b]
        both = jnp.concatenate(
            [
                jnp.concatenate([query * first_head, bias_q * first_head], axis=1),
                jnp.concatenate([query * second_head, bias_q * second_head], axis=1),
            ],
            axis=0,
        )
        scores, near_values = [], []
        for e in range(attn_slots):
            pos = place(attn_cols[b, e])
            at = lax.div(pos, blocks) * (2 * blocks) + lax.rem(pos, blocks)
            key = jnp.concatenate([kv[at], bk[pos]], axis=1)
            near_values.append(kv[at + blocks])
            score = dot_t(both, key)
            scores.append(jnp.where(e < count, score, -1e30))
        scores = jnp.concatenate(scores, axis=1)
        top = jnp.max(scores, axis=1, keepdims=True)
        expo = jnp.exp2((scores - top) * (LOG2E * HD ** (-0.5)))
        weights = (expo * (1.0 / jnp.sum(expo, axis=1, keepdims=True))).astype(jnp.bfloat16)
        mixed = dot(weights, jnp.concatenate(near_values, axis=0))
        attended = jnp.where(lane < HD, mixed[:BS], mixed[BS:]).astype(jnp.bfloat16)
        term = dot(attended, w_out[...]).astype(jnp.bfloat16)
        for p in range(n_feat):
            stage[b * n_feat + p] = term[:, p * BS : (p + 1) * BS]
        start(out_copies(b))
        return carry

    lax.fori_loop(0, blocks, attend, 0)

    def finish(b, carry):
        copies = out_copies(b)
        wait_recv(copies)
        total_out = stage[b * n_feat + me_feat].astype(jnp.float32)
        for i in range(n_feat - 1):
            total_out += landed[b * (n_feat - 1) + i].astype(jnp.float32)
        new_nodes[pl.ds(pl.multiple_of(b * BS, BS), BS), :] = total_out.astype(jnp.bfloat16)
        for copy in copies:
            copy.wait_send()
        return carry

    lax.fori_loop(0, blocks, finish, 0)
    for copies in (state_copies, bw_copies, one_copies, f1_copies, kv_copies, f2_copies, bk_copies):
        for copy in copies:
            copy.wait_send()


def on_device(
    nodes,
    walk_state,
    walk_values,
    walk_cols,
    walk_count,
    attn_cols,
    attn_count,
    w_query,
    w_key,
    w_value,
    bias_query,
    bias_key,
    w_out,
):
    n_dom, n_feat = lax.axis_size("dom"), lax.axis_size("feat")
    blocks, walk_slots = walk_values.shape[:2]
    attn_slots = attn_cols.shape[1]
    rows, width = nodes.shape[0], w_out.shape[1] // n_feat
    half = blocks // 2
    wide = 2 * R + 1
    bf16 = jnp.bfloat16
    dma = pltpu.SemaphoreType.DMA
    smem = pl.BlockSpec(memory_space=pltpu.SMEM)
    vmem = pl.BlockSpec(memory_space=pltpu.VMEM)
    sizes = (n_dom, n_feat, blocks, walk_slots, attn_slots)
    return pl.pallas_call(
        functools.partial(kernel, sizes),
        out_shape=(
            jax.ShapeDtypeStruct((rows, width), bf16),
            jax.ShapeDtypeStruct(walk_state.shape, bf16),
        ),
        in_specs=[smem] * 4 + [vmem] * 9,
        out_specs=(vmem, vmem),
        scratch_shapes=[
            pltpu.VMEM((wide * half, BS, BS), bf16),
            pltpu.VMEM((wide * half, BS, BS), bf16),
            pltpu.VMEM((wide * 2 * blocks, BS, BS), bf16),
            pltpu.VMEM((wide * blocks, BS, BS), bf16),
            pltpu.VMEM((n_feat * half, BS, BS), bf16),
            pltpu.VMEM((n_feat * half, BS, BS), bf16),
            pltpu.VMEM((n_feat, 2, 2, HD, BS), bf16),
            pltpu.VMEM((n_feat, 2, 2 * BS, 2 * BS), bf16),
            pltpu.VMEM((blocks, BS, BS), bf16),
            pltpu.VMEM((blocks, BS, BS), bf16),
            pltpu.VMEM((blocks * n_feat, BS, BS), bf16),
            pltpu.VMEM((blocks * (n_feat - 1), BS, BS), bf16),
            dma((2 * R,)),
            dma((2 * R,)),
            dma((2 * R,)),
            dma((2 * R,)),
            dma((2 * R,)),
            dma((2 * R,)),
            dma((2 * R,)),
            dma((2 * R,)),
            dma((n_feat - 1,)),
            dma((n_feat - 1,)),
            dma((n_feat - 1,)),
            dma((n_feat - 1,)),
            dma((2, n_feat - 1)),
            dma((2, n_feat - 1)),
            dma((blocks, n_feat - 1)),
            dma((blocks, n_feat - 1)),
        ],
        compiler_params=pltpu.CompilerParams(
            collective_id=0, has_side_effects=True, vmem_limit_bytes=40 * 1024 * 1024
        ),
    )(
        walk_cols,
        walk_count,
        attn_cols,
        attn_count,
        nodes,
        walk_state,
        walk_values,
        w_query,
        w_key,
        w_value,
        bias_query,
        bias_key,
        w_out,
    )


def solution(mesh):
    placed = (
        P("dom", None),
        P("dom", "feat"),
        P("dom", None, None, None),
        P("dom", None),
        P("dom"),
        P("dom", None),
        P("dom"),
        P(None, "feat"),
        P(None, "feat"),
        P(None, "feat"),
        P(None, "feat", None),
        P(None, "feat", None),
        P("feat", None),
    )
    return jax.shard_map(
        on_device,
        mesh=mesh,
        in_specs=placed,
        out_specs=(P("dom", "feat"), P("dom", "feat")),
        check_vma=False,
    )
```

```python
import functools

import jax
import jax.numpy as jnp
from jax import lax
from jax.experimental import pallas as pl
from jax.experimental.pallas import tpu as pltpu
from jax.sharding import PartitionSpec as P

HD = 64
BS = 128
R = 2
MESH = pl.DeviceIdType.MESH
LOG2E = 1.4426950408889634


def dot(left, right):
    return jnp.dot(left, right, preferred_element_type=jnp.float32)


def dot_t(left, right):
    return lax.dot_general(
        left, right, (((1,), (1,)), ((), ())), preferred_element_type=jnp.float32
    )


def kernel(
    sizes,
    walk_cols_hbm,
    walk_count_hbm,
    attn_cols_hbm,
    attn_count_hbm,
    nodes_hbm,
    walk_state_hbm,
    walk_values_hbm,
    w_query_hbm,
    w_key_hbm,
    w_value_hbm,
    bias_query_hbm,
    bias_key_hbm,
    w_out_hbm,
    new_nodes,
    walk_next,
    walk_cols,
    walk_count,
    attn_cols,
    attn_count,
    walk_state,
    walk_values,
    w_all,
    bias_maps,
    w_out,
    nwin,
    win0,
    win1,
    kv,
    bk,
    f1,
    f2,
    bw,
    wbd,
    queries,
    biasq,
    stage,
    landed,
    state_send,
    state_recv,
    one_send,
    one_recv,
    kv_send,
    kv_recv,
    bk_send,
    bk_recv,
    f1_send,
    f1_recv,
    f2_send,
    f2_recv,
    bw_send,
    bw_recv,
    out_send,
    out_recv,
    node_send,
    node_recv,
    sib_send,
    sib_recv,
    far_send,
    far_recv,
    relay_send,
    relay_recv,
    local,
):
    n_dom, n_feat, blocks, walk_slots, attn_slots = sizes
    half = blocks // 2
    window_blocks = (2 * R + 1) * blocks
    total = n_dom * blocks
    me_dom = lax.axis_index("dom")
    me_feat = lax.axis_index("feat")
    first = (me_dom - R) * blocks
    side = 1 - 2 * lax.rem(me_dom, 2)
    offsets = (side, R, -R, -side)
    arrivals = (R + side, 0, 2 * R, R - side)
    near = [lax.rem(me_dom + o + n_dom, n_dom) for o in offsets]
    sibling = me_feat + 1 - 2 * lax.rem(me_feat, 2)
    across = lax.rem(me_feat + 2, n_feat)
    diagonal = lax.rem(sibling + 2, n_feat)
    loads = [
        pltpu.make_async_copy(source, target, local.at[i])
        for i, (source, target) in enumerate(
            (
                (walk_state_hbm, walk_state),
                (bias_query_hbm, bias_maps.at[0]),
                (bias_key_hbm, bias_maps.at[1]),
                (nodes_hbm, nwin.at[pl.ds(R * n_feat, n_feat)]),
                (w_query_hbm, w_all.at[:, pl.ds(0, BS)]),
                (w_key_hbm, w_all.at[:, pl.ds(BS, BS)]),
                (w_value_hbm, w_all.at[:, pl.ds(2 * BS, BS)]),
                (walk_cols_hbm, walk_cols),
                (walk_count_hbm, walk_count),
                (walk_values_hbm, walk_values),
                (w_out_hbm, w_out),
                (attn_cols_hbm, attn_cols),
                (attn_count_hbm, attn_count),
            )
        )
    ]
    for load in loads:
        load.start()
    peers = [lax.rem(me_feat + d, n_feat) for d in range(1, n_feat)]
    lane = lax.broadcasted_iota(jnp.int32, (1, BS), 1)
    lane_half = lax.div(lane, HD)

    def place(block_id):
        pos = lax.rem(block_id - first + total, total)
        return jnp.minimum(pos, window_blocks - 1)

    def to_dom(buffer, per, send, recv):
        copies = []
        for i, o in enumerate(offsets):
            copies.append(
                pltpu.make_async_remote_copy(
                    src_ref=buffer.at[pl.ds(R * per, per)],
                    dst_ref=buffer.at[pl.ds((R - o) * per, per)],
                    send_sem=send.at[i],
                    recv_sem=recv.at[i],
                    device_id={"dom": near[i]},
                    device_id_type=MESH,
                )
            )
        return copies

    def to_feat(buffer, per, send, recv):
        copies = []
        mine = pl.ds(me_feat * per, per)
        for i, peer in enumerate(peers):
            copies.append(
                pltpu.make_async_remote_copy(
                    src_ref=buffer.at[mine],
                    dst_ref=buffer.at[mine],
                    send_sem=send.at[i],
                    recv_sem=recv.at[i],
                    device_id={"feat": peer},
                    device_id_type=MESH,
                )
            )
        return copies

    def start(copies):
        for copy in copies:
            copy.start()

    def wait_recv(copies):
        for copy in copies:
            copy.wait_recv()

    loads[0].wait()
    for j in range(half):
        columns = jnp.concatenate(
            [
                walk_state[:, j * BS : (j + 1) * BS],
                walk_state[:, (j + half) * BS : (j + half + 1) * BS],
            ],
            axis=0,
        )
        win0[R * half + j] = columns.T

    barrier = pltpu.get_barrier_semaphore()
    for device in near:
        pl.semaphore_signal(barrier, inc=1, device_id={"dom": device}, device_id_type=MESH)
    for device in peers:
        pl.semaphore_signal(barrier, inc=1, device_id={"feat": device}, device_id_type=MESH)
    pl.semaphore_wait(barrier, len(near) + len(peers))

    state_copies = to_dom(win0, half, state_send, state_recv)
    start(state_copies)
    loads[1].wait()
    loads[2].wait()
    bw_copies = []
    for t in range(2):
        for i, peer in enumerate(peers):
            bw_copies.append(
                pltpu.make_async_remote_copy(
                    src_ref=bias_maps.at[t, :, :, pl.ds(pl.multiple_of(peer * BS, BS), BS)],
                    dst_ref=bw.at[me_feat, t],
                    send_sem=bw_send.at[t, i],
                    recv_sem=bw_recv.at[t, i],
                    device_id={"feat": peer},
                    device_id_type=MESH,
                )
            )
    start(bw_copies)

    for i in range(3, 7):
        loads[i].wait()
    per = blocks // n_feat

    def project(i, carry):
        product = dot(nwin[R * n_feat + i], w_all[...]).astype(jnp.bfloat16)
        queries[pl.ds(per * i, per)] = product[:, :BS].reshape(per, BS, BS)
        kv[pl.ds(2 * R * blocks + per * i, per)] = product[:, BS : 2 * BS].reshape(per, BS, BS)
        kv[pl.ds((2 * R + 1) * blocks + per * i, per)] = product[:, 2 * BS :].reshape(per, BS, BS)
        return carry

    lax.fori_loop(0, n_feat, project, 0)

    def project_near(slot, quarter):
        product = dot(nwin[slot * n_feat + quarter], w_all[:, BS:]).astype(jnp.bfloat16)
        at = slot * 2 * blocks + per * quarter
        kv[pl.ds(at, per)] = product[:, :BS].reshape(per, BS, BS)
        kv[pl.ds(at + blocks, per)] = product[:, BS:].reshape(per, BS, BS)

    def walk_rows(window, b):
        count = walk_count[b]
        parts = []
        for e in range(walk_slots):
            pos = place(walk_cols[b, e])
            part = lax.div(pos, blocks)
            block = lax.rem(pos, blocks)
            column_half = jnp.where(e < count, lax.div(block, half), 2)
            keep = jnp.where(lane_half == column_half, 1.0, 0.0).astype(jnp.bfloat16)
            parts.append(window[part * half + lax.rem(block, half)] * keep)
        left = jnp.concatenate([walk_values[b, e] for e in range(walk_slots)], axis=1)
        both = dot(left, jnp.concatenate(parts, axis=0))
        return both + pltpu.roll(both, HD, 1)

    def walk_pair(window, j):
        low = walk_rows(window, j)
        high = walk_rows(window, j + half)
        return jnp.where(lane < HD, low, high).astype(jnp.bfloat16)

    for i in range(7, 10):
        loads[i].wait()
    wait_recv(state_copies)
    node_copies = {}
    for i in range(1, 4):
        node_copies[i] = pltpu.make_async_remote_copy(
            src_ref=nwin.at[R * n_feat + me_feat],
            dst_ref=nwin.at[(R - offsets[i]) * n_feat + me_feat],
            send_sem=node_send.at[i],
            recv_sem=node_recv.at[i],
            device_id={"dom": near[i]},
            device_id_type=MESH,
        )
    kv_copy = pltpu.make_async_remote_copy(
        src_ref=kv.at[pl.ds(R * 2 * blocks, 2 * blocks)],
        dst_ref=kv.at[pl.ds((R - side) * 2 * blocks, 2 * blocks)],
        send_sem=kv_send,
        recv_sem=kv_recv,
        device_id={"dom": near[0]},
        device_id_type=MESH,
    )

    def step_one(j, carry):
        pair = walk_pair(win0, j)
        win1[R * half + j] = pair
        f1[me_feat * half + j] = pair
        return carry

    lax.fori_loop(0, half, step_one, 0)
    one_copies = to_dom(win1, half, one_send, one_recv)
    start(one_copies)
    f1_copies = to_feat(f1, half, f1_send, f1_recv)
    start(f1_copies)
    start(node_copies.values())
    kv_copy.start()

    own = pl.ds(pl.multiple_of(me_feat * BS, BS), BS)
    bw[me_feat, 0] = bias_maps[0, :, :, own]
    bw[me_feat, 1] = bias_maps[1, :, :, own]
    wait_recv(bw_copies)
    zero = jnp.zeros((HD, BS), jnp.bfloat16)

    def spread(g, carry):
        for t in range(2):
            for s in range(2):
                weight = bw[g, t, s]
                wbd[g, t, pl.ds(s * BS, HD), :] = jnp.concatenate([weight, zero], axis=1)
                wbd[g, t, pl.ds(s * BS + HD, HD), :] = jnp.concatenate([zero, weight], axis=1)
        return carry

    lax.fori_loop(0, n_feat, spread, 0)

    wait_recv(one_copies)

    def step_two(j, carry):
        pair = walk_pair(win1, j)
        f2[me_feat * half + j] = pair
        columns = pair.T
        walk_next[:, pl.ds(pl.multiple_of(j * BS, BS), BS)] = columns[:HD]
        walk_next[:, pl.ds(pl.multiple_of((j + half) * BS, BS), BS)] = columns[HD:]
        return carry

    lax.fori_loop(0, half, step_two, 0)
    f2_copies = to_feat(f2, half, f2_send, f2_recv)
    start(f2_copies)
    wait_recv(f1_copies)
    wait_recv(f2_copies)

    def bias(j, carry):
        sums = [None, None]
        for g in range(n_feat):
            feats = jnp.concatenate([f1[g * half + j], f2[g * half + j]], axis=1)
            for t in range(2):
                term = dot(feats, wbd[g, t]).astype(jnp.bfloat16).astype(jnp.float32)
                sums[t] = term if sums[t] is None else sums[t] + term
        bias_q, bias_k = sums[0].astype(jnp.bfloat16), sums[1].astype(jnp.bfloat16)
        biasq[j] = bias_q[:, :BS]
        biasq[j + half] = bias_q[:, BS:]
        bk[R * blocks + j] = bias_k[:, :BS]
        bk[R * blocks + j + half] = bias_k[:, BS:]
        return carry

    lax.fori_loop(0, half, bias, 0)
    bk_copies = to_dom(bk, blocks, bk_send, bk_recv)
    start(bk_copies)

    def pass_on(i, quarter, target, send, recv):
        return pltpu.make_async_remote_copy(
            src_ref=nwin.at[arrivals[i] * n_feat + quarter],
            dst_ref=nwin.at[arrivals[i] * n_feat + quarter],
            send_sem=send.at[i],
            recv_sem=recv.at[i],
            device_id={"feat": target},
            device_id_type=MESH,
        )

    shared = []
    far, beside, relayed = {}, {}, {}
    for i in range(1, 4):
        node_copies[i].wait_recv()
        far[i] = pass_on(i, me_feat, across, far_send, far_recv)
        beside[i] = pass_on(i, me_feat, sibling, sib_send, sib_recv)
        relayed[i] = pass_on(i, across, sibling, relay_send, relay_recv)
        far[i].start()
        beside[i].start()
        project_near(arrivals[i], me_feat)
    for i in range(1, 4):
        far[i].wait_recv()
        relayed[i].start()
        project_near(arrivals[i], across)
        beside[i].wait_recv()
        project_near(arrivals[i], sibling)
    for i in range(1, 4):
        relayed[i].wait_recv()
        project_near(arrivals[i], diagonal)
    for copies in (far, beside, relayed):
        shared += copies.values()
    kv_copy.wait_recv()
    wait_recv(bk_copies)
    for i in range(10, 13):
        loads[i].wait()

    def out_copies(b):
        return [
            pltpu.make_async_remote_copy(
                src_ref=stage.at[b * n_feat + peer],
                dst_ref=landed.at[b * (n_feat - 1) + i],
                send_sem=out_send.at[b, i],
                recv_sem=out_recv.at[b, i],
                device_id={"feat": peer},
                device_id_type=MESH,
            )
            for i, peer in enumerate(peers)
        ]

    first_head = jnp.where(lane < HD, 1.0, 0.0).astype(jnp.bfloat16)
    second_head = jnp.where(lane < HD, 0.0, 1.0).astype(jnp.bfloat16)

    def attend(b, carry):
        count = attn_count[b]
        query, bias_q = queries[b], biasq[b]
        both = jnp.concatenate(
            [
                jnp.concatenate([query * first_head, bias_q * first_head], axis=1),
                jnp.concatenate([query * second_head, bias_q * second_head], axis=1),
            ],
            axis=0,
        )
        scores, near_values = [], []
        for e in range(attn_slots):
            pos = place(attn_cols[b, e])
            at = lax.div(pos, blocks) * (2 * blocks) + lax.rem(pos, blocks)
            key = jnp.concatenate([kv[at], bk[pos]], axis=1)
            near_values.append(kv[at + blocks])
            score = dot_t(both, key)
            scores.append(jnp.where(e < count, score, -1e30))
        scores = jnp.concatenate(scores, axis=1)
        top = jnp.max(scores, axis=1, keepdims=True)
        expo = jnp.exp2((scores - top) * (LOG2E * HD ** (-0.5)))
        weights = (expo * (1.0 / jnp.sum(expo, axis=1, keepdims=True))).astype(jnp.bfloat16)
        mixed = dot(weights, jnp.concatenate(near_values, axis=0))
        attended = jnp.where(lane < HD, mixed[:BS], mixed[BS:]).astype(jnp.bfloat16)
        term = dot(attended, w_out[...]).astype(jnp.bfloat16)
        for p in range(n_feat):
            stage[b * n_feat + p] = term[:, p * BS : (p + 1) * BS]
        start(out_copies(b))
        return carry

    lax.fori_loop(0, blocks, attend, 0)

    def finish(b, carry):
        copies = out_copies(b)
        wait_recv(copies)
        total_out = stage[b * n_feat + me_feat].astype(jnp.float32)
        for i in range(n_feat - 1):
            total_out += landed[b * (n_feat - 1) + i].astype(jnp.float32)
        new_nodes[pl.ds(pl.multiple_of(b * BS, BS), BS), :] = total_out.astype(jnp.bfloat16)
        for copy in copies:
            copy.wait_send()
        return carry

    lax.fori_loop(0, blocks, finish, 0)
    for copies in (state_copies, bw_copies, one_copies, f1_copies, f2_copies, bk_copies):
        for copy in copies:
            copy.wait_send()
    for copy in [kv_copy, *node_copies.values(), *shared]:
        copy.wait_send()


def on_device(
    nodes,
    walk_state,
    walk_values,
    walk_cols,
    walk_count,
    attn_cols,
    attn_count,
    w_query,
    w_key,
    w_value,
    bias_query,
    bias_key,
    w_out,
):
    n_dom, n_feat = lax.axis_size("dom"), lax.axis_size("feat")
    blocks, walk_slots = walk_values.shape[:2]
    attn_slots = attn_cols.shape[1]
    rows, width = nodes.shape[0], w_out.shape[1] // n_feat
    half = blocks // 2
    wide = 2 * R + 1
    bf16 = jnp.bfloat16
    dma = pltpu.SemaphoreType.DMA
    hbm = pl.BlockSpec(memory_space=pltpu.HBM)
    vmem = pl.BlockSpec(memory_space=pltpu.VMEM)
    sizes = (n_dom, n_feat, blocks, walk_slots, attn_slots)
    out, next_columns = pl.pallas_call(
        functools.partial(kernel, sizes),
        out_shape=(
            jax.ShapeDtypeStruct((rows, width), bf16),
            jax.ShapeDtypeStruct(walk_state.shape[::-1], bf16),
        ),
        in_specs=[hbm] * 13,
        out_specs=(vmem, vmem),
        scratch_shapes=[
            pltpu.SMEM(walk_cols.shape, jnp.int32),
            pltpu.SMEM(walk_count.shape, jnp.int32),
            pltpu.SMEM(attn_cols.shape, jnp.int32),
            pltpu.SMEM(attn_count.shape, jnp.int32),
            pltpu.VMEM(walk_state.shape[::-1], bf16),
            pltpu.VMEM(walk_values.shape, bf16),
            pltpu.VMEM((nodes.shape[1], 3 * BS), bf16),
            pltpu.VMEM((2, *bias_query.shape), bf16),
            pltpu.VMEM(w_out.shape, bf16),
            pltpu.VMEM((wide * n_feat, rows // n_feat, nodes.shape[1]), bf16),
            pltpu.VMEM((wide * half, BS, BS), bf16),
            pltpu.VMEM((wide * half, BS, BS), bf16),
            pltpu.VMEM((wide * 2 * blocks, BS, BS), bf16),
            pltpu.VMEM((wide * blocks, BS, BS), bf16),
            pltpu.VMEM((n_feat * half, BS, BS), bf16),
            pltpu.VMEM((n_feat * half, BS, BS), bf16),
            pltpu.VMEM((n_feat, 2, 2, HD, BS), bf16),
            pltpu.VMEM((n_feat, 2, 2 * BS, 2 * BS), bf16),
            pltpu.VMEM((blocks, BS, BS), bf16),
            pltpu.VMEM((blocks, BS, BS), bf16),
            pltpu.VMEM((blocks * n_feat, BS, BS), bf16),
            pltpu.VMEM((blocks * (n_feat - 1), BS, BS), bf16),
            dma((2 * R,)),
            dma((2 * R,)),
            dma((2 * R,)),
            dma((2 * R,)),
            dma(()),
            dma(()),
            dma((2 * R,)),
            dma((2 * R,)),
            dma((n_feat - 1,)),
            dma((n_feat - 1,)),
            dma((n_feat - 1,)),
            dma((n_feat - 1,)),
            dma((2, n_feat - 1)),
            dma((2, n_feat - 1)),
            dma((blocks, n_feat - 1)),
            dma((blocks, n_feat - 1)),
            dma((2 * R,)),
            dma((2 * R,)),
            dma((2 * R,)),
            dma((2 * R,)),
            dma((2 * R,)),
            dma((2 * R,)),
            dma((2 * R,)),
            dma((2 * R,)),
            dma((13,)),
        ],
        compiler_params=pltpu.CompilerParams(
            collective_id=0, has_side_effects=True, vmem_limit_bytes=63 * 1024 * 1024
        ),
    )(
        walk_cols,
        walk_count,
        attn_cols,
        attn_count,
        nodes.reshape(n_feat, rows // n_feat, nodes.shape[1]),
        walk_state.T,
        walk_values,
        w_query,
        w_key,
        w_value,
        bias_query,
        bias_key,
        w_out,
    )
    return out, next_columns.T


def solution(mesh):
    placed = (
        P("dom", None),
        P("dom", "feat"),
        P("dom", None, None, None),
        P("dom", None),
        P("dom"),
        P("dom", None),
        P("dom"),
        P(None, "feat"),
        P(None, "feat"),
        P(None, "feat"),
        P(None, "feat", None),
        P(None, "feat", None),
        P("feat", None),
    )
    return jax.shard_map(
        on_device,
        mesh=mesh,
        in_specs=placed,
        out_specs=(P("dom", "feat"), P("dom", "feat")),
        check_vma=False,
    )
```

```python
import functools

import jax
import jax.numpy as jnp
from jax import lax
from jax.experimental import pallas as pl
from jax.experimental.pallas import tpu as pltpu
from jax.sharding import PartitionSpec as P

HD = 64
BS = 128
R = 2
MESH = pl.DeviceIdType.MESH
LOG2E = 1.4426950408889634


def dot(left, right):
    return jnp.dot(left, right, preferred_element_type=jnp.float32)


def dot_t(left, right):
    return lax.dot_general(
        left, right, (((1,), (1,)), ((), ())), preferred_element_type=jnp.float32
    )


def kernel(
    sizes,
    walk_cols_hbm,
    walk_count_hbm,
    attn_cols_hbm,
    attn_count_hbm,
    nodes_hbm,
    walk_state_hbm,
    walk_values_hbm,
    w_query_hbm,
    w_key_hbm,
    w_value_hbm,
    bias_query_hbm,
    bias_key_hbm,
    w_out_hbm,
    new_nodes,
    walk_next,
    walk_cols,
    walk_count,
    attn_cols,
    attn_count,
    walk_state,
    walk_values,
    w_all,
    bias_maps,
    w_out,
    nwin,
    win0,
    win1,
    kv,
    bk,
    f1,
    f2,
    bw,
    wbd,
    queries,
    biasq,
    att,
    wo,
    state_send,
    state_recv,
    one_send,
    one_recv,
    kv_send,
    kv_recv,
    bk_send,
    bk_recv,
    f1_send,
    f1_recv,
    f2_send,
    f2_recv,
    bw_send,
    bw_recv,
    out_send,
    out_recv,
    node_send,
    node_recv,
    sib_send,
    sib_recv,
    far_send,
    far_recv,
    relay_send,
    relay_recv,
    local,
    wo_send,
    wo_recv,
):
    n_dom, n_feat, blocks, walk_slots, attn_slots = sizes
    half = blocks // 2
    window_blocks = (2 * R + 1) * blocks
    total = n_dom * blocks
    me_dom = lax.axis_index("dom")
    me_feat = lax.axis_index("feat")
    first = (me_dom - R) * blocks
    side = 1 - 2 * lax.rem(me_dom, 2)
    offsets = (side, R, -R, -side)
    arrivals = (R + side, 0, 2 * R, R - side)
    near = [lax.rem(me_dom + o + n_dom, n_dom) for o in offsets]
    sibling = me_feat + 1 - 2 * lax.rem(me_feat, 2)
    across = lax.rem(me_feat + 2, n_feat)
    diagonal = lax.rem(sibling + 2, n_feat)
    loads = [
        pltpu.make_async_copy(source, target, local.at[i])
        for i, (source, target) in enumerate(
            (
                (walk_state_hbm, walk_state),
                (bias_query_hbm, bias_maps.at[0]),
                (bias_key_hbm, bias_maps.at[1]),
                (nodes_hbm, nwin.at[pl.ds(R * n_feat, n_feat)]),
                (w_query_hbm, w_all.at[:, pl.ds(0, BS)]),
                (w_key_hbm, w_all.at[:, pl.ds(BS, BS)]),
                (w_value_hbm, w_all.at[:, pl.ds(2 * BS, BS)]),
                (walk_cols_hbm, walk_cols),
                (walk_count_hbm, walk_count),
                (walk_values_hbm, walk_values),
                (w_out_hbm, w_out),
                (attn_cols_hbm, attn_cols),
                (attn_count_hbm, attn_count),
            )
        )
    ]
    for load in loads:
        load.start()
    peers = [lax.rem(me_feat + d, n_feat) for d in range(1, n_feat)]
    lane = lax.broadcasted_iota(jnp.int32, (1, BS), 1)
    lane_half = lax.div(lane, HD)

    def place(block_id):
        pos = lax.rem(block_id - first + total, total)
        return jnp.minimum(pos, window_blocks - 1)

    def to_dom(buffer, per, send, recv):
        copies = []
        for i, o in enumerate(offsets):
            copies.append(
                pltpu.make_async_remote_copy(
                    src_ref=buffer.at[pl.ds(R * per, per)],
                    dst_ref=buffer.at[pl.ds((R - o) * per, per)],
                    send_sem=send.at[i],
                    recv_sem=recv.at[i],
                    device_id={"dom": near[i]},
                    device_id_type=MESH,
                )
            )
        return copies

    def to_feat(buffer, per, send, recv):
        copies = []
        mine = pl.ds(me_feat * per, per)
        for i, peer in enumerate(peers):
            copies.append(
                pltpu.make_async_remote_copy(
                    src_ref=buffer.at[mine],
                    dst_ref=buffer.at[mine],
                    send_sem=send.at[i],
                    recv_sem=recv.at[i],
                    device_id={"feat": peer},
                    device_id_type=MESH,
                )
            )
        return copies

    def start(copies):
        for copy in copies:
            copy.start()

    def wait_recv(copies):
        for copy in copies:
            copy.wait_recv()

    loads[0].wait()
    for j in range(half):
        columns = jnp.concatenate(
            [
                walk_state[:, j * BS : (j + 1) * BS],
                walk_state[:, (j + half) * BS : (j + half + 1) * BS],
            ],
            axis=0,
        )
        win0[R * half + j] = columns.T

    barrier = pltpu.get_barrier_semaphore()
    for device in near:
        pl.semaphore_signal(barrier, inc=1, device_id={"dom": device}, device_id_type=MESH)
    for device in peers:
        pl.semaphore_signal(barrier, inc=1, device_id={"feat": device}, device_id_type=MESH)
    pl.semaphore_wait(barrier, len(near) + len(peers))

    state_copies = to_dom(win0, half, state_send, state_recv)
    start(state_copies)
    loads[1].wait()
    loads[2].wait()
    bw_copies = []
    for t in range(2):
        for i, peer in enumerate(peers):
            bw_copies.append(
                pltpu.make_async_remote_copy(
                    src_ref=bias_maps.at[t, :, :, pl.ds(pl.multiple_of(peer * BS, BS), BS)],
                    dst_ref=bw.at[me_feat, t],
                    send_sem=bw_send.at[t, i],
                    recv_sem=bw_recv.at[t, i],
                    device_id={"feat": peer},
                    device_id_type=MESH,
                )
            )
    start(bw_copies)
    loads[10].wait()
    wo_copies = [
        pltpu.make_async_remote_copy(
            src_ref=w_out.at[:, pl.ds(pl.multiple_of(peer * BS, BS), BS)],
            dst_ref=wo.at[me_feat],
            send_sem=wo_send.at[i],
            recv_sem=wo_recv.at[i],
            device_id={"feat": peer},
            device_id_type=MESH,
        )
        for i, peer in enumerate(peers)
    ]
    start(wo_copies)

    for i in range(3, 7):
        loads[i].wait()
    per = blocks // n_feat

    def project(i, carry):
        product = dot(nwin[R * n_feat + i], w_all[...]).astype(jnp.bfloat16)
        queries[pl.ds(per * i, per)] = product[:, :BS].reshape(per, BS, BS)
        kv[pl.ds(2 * R * blocks + per * i, per)] = product[:, BS : 2 * BS].reshape(per, BS, BS)
        kv[pl.ds((2 * R + 1) * blocks + per * i, per)] = product[:, 2 * BS :].reshape(per, BS, BS)
        return carry

    lax.fori_loop(0, n_feat, project, 0)

    def project_near(slot, quarter):
        product = dot(nwin[slot * n_feat + quarter], w_all[:, BS:]).astype(jnp.bfloat16)
        at = slot * 2 * blocks + per * quarter
        kv[pl.ds(at, per)] = product[:, :BS].reshape(per, BS, BS)
        kv[pl.ds(at + blocks, per)] = product[:, BS:].reshape(per, BS, BS)

    def walk_rows(window, b):
        count = walk_count[b]
        parts = []
        for e in range(walk_slots):
            pos = place(walk_cols[b, e])
            part = lax.div(pos, blocks)
            block = lax.rem(pos, blocks)
            column_half = jnp.where(e < count, lax.div(block, half), 2)
            keep = jnp.where(lane_half == column_half, 1.0, 0.0).astype(jnp.bfloat16)
            parts.append(window[part * half + lax.rem(block, half)] * keep)
        left = jnp.concatenate([walk_values[b, e] for e in range(walk_slots)], axis=1)
        both = dot(left, jnp.concatenate(parts, axis=0))
        return both + pltpu.roll(both, HD, 1)

    def walk_pair(window, j):
        low = walk_rows(window, j)
        high = walk_rows(window, j + half)
        return jnp.where(lane < HD, low, high).astype(jnp.bfloat16)

    for i in range(7, 10):
        loads[i].wait()
    wait_recv(state_copies)
    node_copies = {}
    for i in range(1, 4):
        node_copies[i] = pltpu.make_async_remote_copy(
            src_ref=nwin.at[R * n_feat + me_feat],
            dst_ref=nwin.at[(R - offsets[i]) * n_feat + me_feat],
            send_sem=node_send.at[i],
            recv_sem=node_recv.at[i],
            device_id={"dom": near[i]},
            device_id_type=MESH,
        )
    kv_copy = pltpu.make_async_remote_copy(
        src_ref=kv.at[pl.ds(R * 2 * blocks, 2 * blocks)],
        dst_ref=kv.at[pl.ds((R - side) * 2 * blocks, 2 * blocks)],
        send_sem=kv_send,
        recv_sem=kv_recv,
        device_id={"dom": near[0]},
        device_id_type=MESH,
    )

    def step_one(j, carry):
        pair = walk_pair(win0, j)
        win1[R * half + j] = pair
        f1[me_feat * half + j] = pair
        return carry

    lax.fori_loop(0, half, step_one, 0)
    one_copies = to_dom(win1, half, one_send, one_recv)
    start(one_copies)
    f1_copies = to_feat(f1, half, f1_send, f1_recv)
    start(f1_copies)
    start(node_copies.values())
    kv_copy.start()

    own = pl.ds(pl.multiple_of(me_feat * BS, BS), BS)
    bw[me_feat, 0] = bias_maps[0, :, :, own]
    bw[me_feat, 1] = bias_maps[1, :, :, own]
    wo[me_feat] = w_out[:, own]
    wait_recv(wo_copies)
    wait_recv(bw_copies)
    zero = jnp.zeros((HD, BS), jnp.bfloat16)

    def spread(g, carry):
        for t in range(2):
            for s in range(2):
                weight = bw[g, t, s]
                wbd[g, t, pl.ds(s * BS, HD), :] = jnp.concatenate([weight, zero], axis=1)
                wbd[g, t, pl.ds(s * BS + HD, HD), :] = jnp.concatenate([zero, weight], axis=1)
        return carry

    lax.fori_loop(0, n_feat, spread, 0)

    wait_recv(one_copies)

    def f2_copies(j):
        at = me_feat * half + j
        return [
            pltpu.make_async_remote_copy(
                src_ref=f2.at[at],
                dst_ref=f2.at[at],
                send_sem=f2_send.at[j, i],
                recv_sem=f2_recv.at[j, i],
                device_id={"feat": peer},
                device_id_type=MESH,
            )
            for i, peer in enumerate(peers)
        ]

    def bk_copies(j):
        return [
            pltpu.make_async_remote_copy(
                src_ref=bk.at[pl.ds(R * blocks + 2 * j, 2)],
                dst_ref=bk.at[pl.ds((R - o) * blocks + 2 * j, 2)],
                send_sem=bk_send.at[j, i],
                recv_sem=bk_recv.at[j, i],
                device_id={"dom": near[i]},
                device_id_type=MESH,
            )
            for i, o in enumerate(offsets)
        ]

    def step_two(j, carry):
        pair = walk_pair(win1, j)
        f2[me_feat * half + j] = pair
        start(f2_copies(j))
        columns = pair.T
        walk_next[:, pl.ds(pl.multiple_of(j * BS, BS), BS)] = columns[:HD]
        walk_next[:, pl.ds(pl.multiple_of((j + half) * BS, BS), BS)] = columns[HD:]
        return carry

    lax.fori_loop(0, half, step_two, 0)
    wait_recv(f1_copies)

    def bias(j, carry):
        wait_recv(f2_copies(j))
        sums = [None, None]
        for g in range(n_feat):
            feats = jnp.concatenate([f1[g * half + j], f2[g * half + j]], axis=1)
            for t in range(2):
                term = dot(feats, wbd[g, t]).astype(jnp.bfloat16).astype(jnp.float32)
                sums[t] = term if sums[t] is None else sums[t] + term
        bias_q, bias_k = sums[0].astype(jnp.bfloat16), sums[1].astype(jnp.bfloat16)
        biasq[j] = bias_q[:, :BS]
        biasq[j + half] = bias_q[:, BS:]
        bk[R * blocks + 2 * j] = bias_k[:, :BS]
        bk[R * blocks + 2 * j + 1] = bias_k[:, BS:]
        start(bk_copies(j))
        return carry

    lax.fori_loop(0, half, bias, 0)

    def pass_on(i, quarter, target, send, recv):
        return pltpu.make_async_remote_copy(
            src_ref=nwin.at[arrivals[i] * n_feat + quarter],
            dst_ref=nwin.at[arrivals[i] * n_feat + quarter],
            send_sem=send.at[i],
            recv_sem=recv.at[i],
            device_id={"feat": target},
            device_id_type=MESH,
        )

    shared = []
    far, beside, relayed = {}, {}, {}
    for i in range(1, 4):
        node_copies[i].wait_recv()
        far[i] = pass_on(i, me_feat, across, far_send, far_recv)
        beside[i] = pass_on(i, me_feat, sibling, sib_send, sib_recv)
        relayed[i] = pass_on(i, across, sibling, relay_send, relay_recv)
        far[i].start()
        beside[i].start()
        project_near(arrivals[i], me_feat)
    for i in range(1, 4):
        far[i].wait_recv()
        relayed[i].start()
        project_near(arrivals[i], across)
        beside[i].wait_recv()
        project_near(arrivals[i], sibling)
    for i in range(1, 4):
        relayed[i].wait_recv()
        project_near(arrivals[i], diagonal)
    for copies in (far, beside, relayed):
        shared += copies.values()
    kv_copy.wait_recv()

    def bk_landed(j, carry):
        wait_recv(bk_copies(j))
        return carry

    lax.fori_loop(0, half, bk_landed, 0)
    loads[11].wait()
    loads[12].wait()

    def att_copies(b):
        moves = ((me_feat, sibling), (me_feat, across), (across, sibling))
        return [
            pltpu.make_async_remote_copy(
                src_ref=att.at[group * blocks + b],
                dst_ref=att.at[group * blocks + b],
                send_sem=out_send.at[b, i],
                recv_sem=out_recv.at[b, i],
                device_id={"feat": target},
                device_id_type=MESH,
            )
            for i, (group, target) in enumerate(moves)
        ]

    def relay(b):
        copies = att_copies(b)
        copies[1].wait_recv()
        copies[2].start()

    first_head = jnp.where(lane < HD, 1.0, 0.0).astype(jnp.bfloat16)
    second_head = jnp.where(lane < HD, 0.0, 1.0).astype(jnp.bfloat16)

    def attend(b, carry):
        count = attn_count[b]
        query, bias_q = queries[b], biasq[b]
        both = jnp.concatenate(
            [
                jnp.concatenate([query * first_head, bias_q * first_head], axis=1),
                jnp.concatenate([query * second_head, bias_q * second_head], axis=1),
            ],
            axis=0,
        )
        scores, near_values = [], []
        for e in range(attn_slots):
            pos = place(attn_cols[b, e])
            part, block = lax.div(pos, blocks), lax.rem(pos, blocks)
            at = part * (2 * blocks) + block
            bias_at = part * blocks + 2 * lax.rem(block, half) + lax.div(block, half)
            key = jnp.concatenate([kv[at], bk[bias_at]], axis=1)
            near_values.append(kv[at + blocks])
            score = dot_t(both, key)
            scores.append(jnp.where(e < count, score, -1e30))
        scores = jnp.concatenate(scores, axis=1)
        top = jnp.max(scores, axis=1, keepdims=True)
        expo = jnp.exp2((scores - top) * (LOG2E * HD ** (-0.5)))
        weights = (expo * (1.0 / jnp.sum(expo, axis=1, keepdims=True))).astype(jnp.bfloat16)
        mixed = dot(weights, jnp.concatenate(near_values, axis=0))
        attended = jnp.where(lane < HD, mixed[:BS], mixed[BS:]).astype(jnp.bfloat16)
        att[me_feat * blocks + b] = attended
        copies = att_copies(b)
        copies[1].start()
        copies[0].start()

        @pl.when(b >= lag)
        def _():
            relay(b - lag)

        return carry

    lag = 2
    lax.fori_loop(0, blocks, attend, 0)

    def relay_rest(b, carry):
        relay(b)
        return carry

    lax.fori_loop(blocks - lag, blocks, relay_rest, 0)

    def finish(b, carry):
        copies = att_copies(b)
        copies[0].wait_recv()
        copies[2].wait_recv()
        total_out = None
        for g in range(n_feat):
            term = dot(att[g * blocks + b], wo[g]).astype(jnp.bfloat16).astype(jnp.float32)
            total_out = term if total_out is None else total_out + term
        new_nodes[pl.ds(pl.multiple_of(b * BS, BS), BS), :] = total_out.astype(jnp.bfloat16)
        for copy in copies:
            copy.wait_send()
        return carry

    lax.fori_loop(0, blocks, finish, 0)

    def drain(j, carry):
        for copy in f2_copies(j) + bk_copies(j):
            copy.wait_send()
        return carry

    lax.fori_loop(0, half, drain, 0)
    for copies in (state_copies, bw_copies, wo_copies, one_copies, f1_copies):
        for copy in copies:
            copy.wait_send()
    for copy in [kv_copy, *node_copies.values(), *shared]:
        copy.wait_send()


def on_device(
    nodes,
    walk_state,
    walk_values,
    walk_cols,
    walk_count,
    attn_cols,
    attn_count,
    w_query,
    w_key,
    w_value,
    bias_query,
    bias_key,
    w_out,
):
    n_dom, n_feat = lax.axis_size("dom"), lax.axis_size("feat")
    blocks, walk_slots = walk_values.shape[:2]
    attn_slots = attn_cols.shape[1]
    rows, width = nodes.shape[0], w_out.shape[1] // n_feat
    half = blocks // 2
    wide = 2 * R + 1
    bf16 = jnp.bfloat16
    dma = pltpu.SemaphoreType.DMA
    hbm = pl.BlockSpec(memory_space=pltpu.HBM)
    vmem = pl.BlockSpec(memory_space=pltpu.VMEM)
    sizes = (n_dom, n_feat, blocks, walk_slots, attn_slots)
    out, next_columns = pl.pallas_call(
        functools.partial(kernel, sizes),
        out_shape=(
            jax.ShapeDtypeStruct((rows, width), bf16),
            jax.ShapeDtypeStruct(walk_state.shape[::-1], bf16),
        ),
        in_specs=[hbm] * 13,
        out_specs=(vmem, vmem),
        scratch_shapes=[
            pltpu.SMEM(walk_cols.shape, jnp.int32),
            pltpu.SMEM(walk_count.shape, jnp.int32),
            pltpu.SMEM(attn_cols.shape, jnp.int32),
            pltpu.SMEM(attn_count.shape, jnp.int32),
            pltpu.VMEM(walk_state.shape[::-1], bf16),
            pltpu.VMEM(walk_values.shape, bf16),
            pltpu.VMEM((nodes.shape[1], 3 * BS), bf16),
            pltpu.VMEM((2, *bias_query.shape), bf16),
            pltpu.VMEM(w_out.shape, bf16),
            pltpu.VMEM((wide * n_feat, rows // n_feat, nodes.shape[1]), bf16),
            pltpu.VMEM((wide * half, BS, BS), bf16),
            pltpu.VMEM((wide * half, BS, BS), bf16),
            pltpu.VMEM((wide * 2 * blocks, BS, BS), bf16),
            pltpu.VMEM((wide * blocks, BS, BS), bf16),
            pltpu.VMEM((n_feat * half, BS, BS), bf16),
            pltpu.VMEM((n_feat * half, BS, BS), bf16),
            pltpu.VMEM((n_feat, 2, 2, HD, BS), bf16),
            pltpu.VMEM((n_feat, 2, 2 * BS, 2 * BS), bf16),
            pltpu.VMEM((blocks, BS, BS), bf16),
            pltpu.VMEM((blocks, BS, BS), bf16),
            pltpu.VMEM((blocks * n_feat, BS, BS), bf16),
            pltpu.VMEM((n_feat, BS, BS), bf16),
            dma((2 * R,)),
            dma((2 * R,)),
            dma((2 * R,)),
            dma((2 * R,)),
            dma(()),
            dma(()),
            dma((half, 2 * R)),
            dma((half, 2 * R)),
            dma((n_feat - 1,)),
            dma((n_feat - 1,)),
            dma((half, n_feat - 1)),
            dma((half, n_feat - 1)),
            dma((2, n_feat - 1)),
            dma((2, n_feat - 1)),
            dma((blocks, n_feat - 1)),
            dma((blocks, n_feat - 1)),
            dma((2 * R,)),
            dma((2 * R,)),
            dma((2 * R,)),
            dma((2 * R,)),
            dma((2 * R,)),
            dma((2 * R,)),
            dma((2 * R,)),
            dma((2 * R,)),
            dma((13,)),
            dma((n_feat - 1,)),
            dma((n_feat - 1,)),
        ],
        compiler_params=pltpu.CompilerParams(
            collective_id=0, has_side_effects=True, vmem_limit_bytes=63 * 1024 * 1024
        ),
    )(
        walk_cols,
        walk_count,
        attn_cols,
        attn_count,
        nodes.reshape(n_feat, rows // n_feat, nodes.shape[1]),
        walk_state.T,
        walk_values,
        w_query,
        w_key,
        w_value,
        bias_query,
        bias_key,
        w_out,
    )
    return out, next_columns.T


def solution(mesh):
    placed = (
        P("dom", None),
        P("dom", "feat"),
        P("dom", None, None, None),
        P("dom", None),
        P("dom"),
        P("dom", None),
        P("dom"),
        P(None, "feat"),
        P(None, "feat"),
        P(None, "feat"),
        P(None, "feat", None),
        P(None, "feat", None),
        P("feat", None),
    )
    return jax.shard_map(
        on_device,
        mesh=mesh,
        in_specs=placed,
        out_specs=(P("dom", "feat"), P("dom", "feat")),
        check_vma=False,
    )
```

```python
import functools

import jax
import jax.numpy as jnp
from jax import lax
from jax.experimental import pallas as pl
from jax.experimental.pallas import tpu as pltpu
from jax.sharding import PartitionSpec as P

HD = 64
BS = 128
R = 2
MESH = pl.DeviceIdType.MESH
LOG2E = 1.4426950408889634


def dot(left, right):
    return jnp.dot(left, right, preferred_element_type=jnp.float32)


def dot_t(left, right):
    return lax.dot_general(
        left, right, (((1,), (1,)), ((), ())), preferred_element_type=jnp.float32
    )


def kernel(
    sizes,
    walk_cols_hbm,
    walk_count_hbm,
    attn_cols_hbm,
    attn_count_hbm,
    nodes_hbm,
    walk_state_hbm,
    walk_values_hbm,
    w_query_hbm,
    w_key_hbm,
    w_value_hbm,
    bias_query_hbm,
    bias_key_hbm,
    w_out_hbm,
    new_nodes,
    walk_next,
    walk_cols,
    walk_count,
    attn_cols,
    attn_count,
    walk_state,
    walk_values,
    w_all,
    bias_maps,
    w_out,
    nwin,
    win0,
    win1,
    kv,
    bk,
    f1,
    f2,
    bw,
    wbd,
    queries,
    biasq,
    stage,
    landed,
    state_send,
    state_recv,
    one_send,
    one_recv,
    kv_send,
    kv_recv,
    bk_send,
    bk_recv,
    f1_send,
    f1_recv,
    f2_send,
    f2_recv,
    bw_send,
    bw_recv,
    out_send,
    out_recv,
    node_send,
    node_recv,
    sib_send,
    sib_recv,
    far_send,
    far_recv,
    relay_send,
    relay_recv,
    local,
):
    n_dom, n_feat, blocks, walk_slots, attn_slots = sizes
    half = blocks // 2
    window_blocks = (2 * R + 1) * blocks
    total = n_dom * blocks
    me_dom = lax.axis_index("dom")
    me_feat = lax.axis_index("feat")
    first = (me_dom - R) * blocks
    side = 1 - 2 * lax.rem(me_dom, 2)
    offsets = (side, R, -R, -side)
    arrivals = (R + side, 0, 2 * R, R - side)
    near = [lax.rem(me_dom + o + n_dom, n_dom) for o in offsets]
    sibling = me_feat + 1 - 2 * lax.rem(me_feat, 2)
    across = lax.rem(me_feat + 2, n_feat)
    diagonal = lax.rem(sibling + 2, n_feat)
    loads = [
        pltpu.make_async_copy(source, target, local.at[i])
        for i, (source, target) in enumerate(
            (
                (walk_state_hbm, walk_state),
                (bias_query_hbm, bias_maps.at[0]),
                (bias_key_hbm, bias_maps.at[1]),
                (nodes_hbm, nwin.at[pl.ds(R * n_feat, n_feat)]),
                (w_query_hbm, w_all.at[:, pl.ds(0, BS)]),
                (w_key_hbm, w_all.at[:, pl.ds(BS, BS)]),
                (w_value_hbm, w_all.at[:, pl.ds(2 * BS, BS)]),
                (walk_cols_hbm, walk_cols),
                (walk_count_hbm, walk_count),
                (walk_values_hbm, walk_values),
                (w_out_hbm, w_out),
                (attn_cols_hbm, attn_cols),
                (attn_count_hbm, attn_count),
            )
        )
    ]
    for load in loads:
        load.start()
    peers = [lax.rem(me_feat + d, n_feat) for d in range(1, n_feat)]
    lane = lax.broadcasted_iota(jnp.int32, (1, BS), 1)
    lane_half = lax.div(lane, HD)

    def place(block_id):
        pos = lax.rem(block_id - first + total, total)
        return jnp.minimum(pos, window_blocks - 1)

    def to_dom(buffer, per, send, recv):
        copies = []
        for i, o in enumerate(offsets):
            copies.append(
                pltpu.make_async_remote_copy(
                    src_ref=buffer.at[pl.ds(R * per, per)],
                    dst_ref=buffer.at[pl.ds((R - o) * per, per)],
                    send_sem=send.at[i],
                    recv_sem=recv.at[i],
                    device_id={"dom": near[i]},
                    device_id_type=MESH,
                )
            )
        return copies

    def to_feat(buffer, per, send, recv):
        copies = []
        mine = pl.ds(me_feat * per, per)
        for i, peer in enumerate(peers):
            copies.append(
                pltpu.make_async_remote_copy(
                    src_ref=buffer.at[mine],
                    dst_ref=buffer.at[mine],
                    send_sem=send.at[i],
                    recv_sem=recv.at[i],
                    device_id={"feat": peer},
                    device_id_type=MESH,
                )
            )
        return copies

    def start(copies):
        for copy in copies:
            copy.start()

    def wait_recv(copies):
        for copy in copies:
            copy.wait_recv()

    loads[0].wait()
    for j in range(half):
        columns = jnp.concatenate(
            [
                walk_state[:, j * BS : (j + 1) * BS],
                walk_state[:, (j + half) * BS : (j + half + 1) * BS],
            ],
            axis=0,
        )
        win0[R * half + j] = columns.T

    barrier = pltpu.get_barrier_semaphore()
    for device in near:
        pl.semaphore_signal(barrier, inc=1, device_id={"dom": device}, device_id_type=MESH)
    for device in peers:
        pl.semaphore_signal(barrier, inc=1, device_id={"feat": device}, device_id_type=MESH)
    pl.semaphore_wait(barrier, len(near) + len(peers))

    state_copies = to_dom(win0, half, state_send, state_recv)
    start(state_copies)
    loads[1].wait()
    loads[2].wait()
    bw_copies = []
    for t in range(2):
        for i, peer in enumerate(peers):
            bw_copies.append(
                pltpu.make_async_remote_copy(
                    src_ref=bias_maps.at[t, :, :, pl.ds(pl.multiple_of(peer * BS, BS), BS)],
                    dst_ref=bw.at[me_feat, t],
                    send_sem=bw_send.at[t, i],
                    recv_sem=bw_recv.at[t, i],
                    device_id={"feat": peer},
                    device_id_type=MESH,
                )
            )
    start(bw_copies)

    for i in range(3, 7):
        loads[i].wait()
    per = blocks // n_feat

    def project(i, carry):
        product = dot(nwin[R * n_feat + i], w_all[...]).astype(jnp.bfloat16)
        queries[pl.ds(per * i, per)] = product[:, :BS].reshape(per, BS, BS)
        kv[pl.ds(2 * R * blocks + per * i, per)] = product[:, BS : 2 * BS].reshape(per, BS, BS)
        kv[pl.ds((2 * R + 1) * blocks + per * i, per)] = product[:, 2 * BS :].reshape(per, BS, BS)
        return carry

    lax.fori_loop(0, n_feat, project, 0)

    def project_near(slot, quarter):
        product = dot(nwin[slot * n_feat + quarter], w_all[:, BS:]).astype(jnp.bfloat16)
        at = slot * 2 * blocks + per * quarter
        kv[pl.ds(at, per)] = product[:, :BS].reshape(per, BS, BS)
        kv[pl.ds(at + blocks, per)] = product[:, BS:].reshape(per, BS, BS)

    def walk_rows(window, b):
        count = walk_count[b]
        parts = []
        for e in range(walk_slots):
            pos = place(walk_cols[b, e])
            part = lax.div(pos, blocks)
            block = lax.rem(pos, blocks)
            column_half = jnp.where(e < count, lax.div(block, half), 2)
            keep = jnp.where(lane_half == column_half, 1.0, 0.0).astype(jnp.bfloat16)
            parts.append(window[part * half + lax.rem(block, half)] * keep)
        left = jnp.concatenate([walk_values[b, e] for e in range(walk_slots)], axis=1)
        both = dot(left, jnp.concatenate(parts, axis=0))
        return both + pltpu.roll(both, HD, 1)

    def walk_pair(window, j):
        low = walk_rows(window, j)
        high = walk_rows(window, j + half)
        return jnp.where(lane < HD, low, high).astype(jnp.bfloat16)

    for i in range(7, 10):
        loads[i].wait()
    wait_recv(state_copies)
    node_copies = {}
    for i in range(1, 4):
        node_copies[i] = pltpu.make_async_remote_copy(
            src_ref=nwin.at[R * n_feat + me_feat],
            dst_ref=nwin.at[(R - offsets[i]) * n_feat + me_feat],
            send_sem=node_send.at[i],
            recv_sem=node_recv.at[i],
            device_id={"dom": near[i]},
            device_id_type=MESH,
        )
    kv_copy = pltpu.make_async_remote_copy(
        src_ref=kv.at[pl.ds(R * 2 * blocks, 2 * blocks)],
        dst_ref=kv.at[pl.ds((R - side) * 2 * blocks, 2 * blocks)],
        send_sem=kv_send,
        recv_sem=kv_recv,
        device_id={"dom": near[0]},
        device_id_type=MESH,
    )

    start(node_copies.values())
    kv_copy.start()

    def step_one(j, carry):
        pair = walk_pair(win0, j)
        win1[R * half + j] = pair
        f1[me_feat * half + j] = pair
        return carry

    lax.fori_loop(0, half, step_one, 0)
    one_copies = to_dom(win1, half, one_send, one_recv)
    start(one_copies)
    f1_copies = to_feat(f1, half, f1_send, f1_recv)
    start(f1_copies)

    own = pl.ds(pl.multiple_of(me_feat * BS, BS), BS)
    bw[me_feat, 0] = bias_maps[0, :, :, own]
    bw[me_feat, 1] = bias_maps[1, :, :, own]
    wait_recv(bw_copies)
    zero = jnp.zeros((HD, BS), jnp.bfloat16)

    def spread(g, carry):
        for t in range(2):
            for s in range(2):
                weight = bw[g, t, s]
                wbd[g, t, pl.ds(s * BS, HD), :] = jnp.concatenate([weight, zero], axis=1)
                wbd[g, t, pl.ds(s * BS + HD, HD), :] = jnp.concatenate([zero, weight], axis=1)
        return carry

    lax.fori_loop(0, n_feat, spread, 0)

    wait_recv(one_copies)

    def step_two(j, carry):
        pair = walk_pair(win1, j)
        f2[me_feat * half + j] = pair
        columns = pair.T
        walk_next[:, pl.ds(pl.multiple_of(j * BS, BS), BS)] = columns[:HD]
        walk_next[:, pl.ds(pl.multiple_of((j + half) * BS, BS), BS)] = columns[HD:]
        return carry

    lax.fori_loop(0, half, step_two, 0)
    f2_copies = to_feat(f2, half, f2_send, f2_recv)
    start(f2_copies)
    wait_recv(f1_copies)
    wait_recv(f2_copies)

    def bias(j, carry):
        sums = [None, None]
        for g in range(n_feat):
            feats = jnp.concatenate([f1[g * half + j], f2[g * half + j]], axis=1)
            for t in range(2):
                term = dot(feats, wbd[g, t]).astype(jnp.bfloat16).astype(jnp.float32)
                sums[t] = term if sums[t] is None else sums[t] + term
        bias_q, bias_k = sums[0].astype(jnp.bfloat16), sums[1].astype(jnp.bfloat16)
        biasq[j] = bias_q[:, :BS]
        biasq[j + half] = bias_q[:, BS:]
        bk[R * blocks + j] = bias_k[:, :BS]
        bk[R * blocks + j + half] = bias_k[:, BS:]
        return carry

    lax.fori_loop(0, half, bias, 0)
    bk_copies = to_dom(bk, blocks, bk_send, bk_recv)
    start(bk_copies)

    def pass_on(i, quarter, target, send, recv):
        return pltpu.make_async_remote_copy(
            src_ref=nwin.at[arrivals[i] * n_feat + quarter],
            dst_ref=nwin.at[arrivals[i] * n_feat + quarter],
            send_sem=send.at[i],
            recv_sem=recv.at[i],
            device_id={"feat": target},
            device_id_type=MESH,
        )

    shared = []
    far, beside, relayed = {}, {}, {}
    for i in range(1, 4):
        node_copies[i].wait_recv()
        far[i] = pass_on(i, me_feat, across, far_send, far_recv)
        beside[i] = pass_on(i, me_feat, sibling, sib_send, sib_recv)
        relayed[i] = pass_on(i, across, sibling, relay_send, relay_recv)
        far[i].start()
        beside[i].start()
        project_near(arrivals[i], me_feat)
    for i in range(1, 4):
        far[i].wait_recv()
        relayed[i].start()
        project_near(arrivals[i], across)
        beside[i].wait_recv()
        project_near(arrivals[i], sibling)
    for i in range(1, 4):
        relayed[i].wait_recv()
        project_near(arrivals[i], diagonal)
    for copies in (far, beside, relayed):
        shared += copies.values()
    kv_copy.wait_recv()
    wait_recv(bk_copies)
    for i in range(10, 13):
        loads[i].wait()

    def out_copies(b):
        return [
            pltpu.make_async_remote_copy(
                src_ref=stage.at[b * n_feat + peer],
                dst_ref=landed.at[b * (n_feat - 1) + i],
                send_sem=out_send.at[b, i],
                recv_sem=out_recv.at[b, i],
                device_id={"feat": peer},
                device_id_type=MESH,
            )
            for i, peer in enumerate(peers)
        ]

    first_head = jnp.where(lane < HD, 1.0, 0.0).astype(jnp.bfloat16)
    second_head = jnp.where(lane < HD, 0.0, 1.0).astype(jnp.bfloat16)

    def attend(b, carry):
        count = attn_count[b]
        query, bias_q = queries[b], biasq[b]
        both = jnp.concatenate(
            [
                jnp.concatenate([query * first_head, bias_q * first_head], axis=1),
                jnp.concatenate([query * second_head, bias_q * second_head], axis=1),
            ],
            axis=0,
        )
        scores, near_values = [], []
        for e in range(attn_slots):
            pos = place(attn_cols[b, e])
            at = lax.div(pos, blocks) * (2 * blocks) + lax.rem(pos, blocks)
            key = jnp.concatenate([kv[at], bk[pos]], axis=1)
            near_values.append(kv[at + blocks])
            score = dot_t(both, key)
            scores.append(jnp.where(e < count, score, -1e30))
        scores = jnp.concatenate(scores, axis=1)
        top = jnp.max(scores, axis=1, keepdims=True)
        expo = jnp.exp2((scores - top) * (LOG2E * HD ** (-0.5)))
        weights = (expo * (1.0 / jnp.sum(expo, axis=1, keepdims=True))).astype(jnp.bfloat16)
        mixed = dot(weights, jnp.concatenate(near_values, axis=0))
        attended = jnp.where(lane < HD, mixed[:BS], mixed[BS:]).astype(jnp.bfloat16)
        term = dot(attended, w_out[...]).astype(jnp.bfloat16)
        for p in range(n_feat):
            stage[b * n_feat + p] = term[:, p * BS : (p + 1) * BS]
        start(out_copies(b))
        return carry

    lax.fori_loop(0, blocks, attend, 0)

    def finish(b, carry):
        copies = out_copies(b)
        wait_recv(copies)
        total_out = stage[b * n_feat + me_feat].astype(jnp.float32)
        for i in range(n_feat - 1):
            total_out += landed[b * (n_feat - 1) + i].astype(jnp.float32)
        new_nodes[pl.ds(pl.multiple_of(b * BS, BS), BS), :] = total_out.astype(jnp.bfloat16)
        for copy in copies:
            copy.wait_send()
        return carry

    lax.fori_loop(0, blocks, finish, 0)
    for copies in (state_copies, bw_copies, one_copies, f1_copies, f2_copies, bk_copies):
        for copy in copies:
            copy.wait_send()
    for copy in [kv_copy, *node_copies.values(), *shared]:
        copy.wait_send()


def on_device(
    nodes,
    walk_state,
    walk_values,
    walk_cols,
    walk_count,
    attn_cols,
    attn_count,
    w_query,
    w_key,
    w_value,
    bias_query,
    bias_key,
    w_out,
):
    n_dom, n_feat = lax.axis_size("dom"), lax.axis_size("feat")
    blocks, walk_slots = walk_values.shape[:2]
    attn_slots = attn_cols.shape[1]
    rows, width = nodes.shape[0], w_out.shape[1] // n_feat
    half = blocks // 2
    wide = 2 * R + 1
    bf16 = jnp.bfloat16
    dma = pltpu.SemaphoreType.DMA
    hbm = pl.BlockSpec(memory_space=pltpu.HBM)
    vmem = pl.BlockSpec(memory_space=pltpu.VMEM)
    sizes = (n_dom, n_feat, blocks, walk_slots, attn_slots)
    out, next_columns = pl.pallas_call(
        functools.partial(kernel, sizes),
        out_shape=(
            jax.ShapeDtypeStruct((rows, width), bf16),
            jax.ShapeDtypeStruct(walk_state.shape[::-1], bf16),
        ),
        in_specs=[hbm] * 13,
        out_specs=(vmem, vmem),
        scratch_shapes=[
            pltpu.SMEM(walk_cols.shape, jnp.int32),
            pltpu.SMEM(walk_count.shape, jnp.int32),
            pltpu.SMEM(attn_cols.shape, jnp.int32),
            pltpu.SMEM(attn_count.shape, jnp.int32),
            pltpu.VMEM(walk_state.shape[::-1], bf16),
            pltpu.VMEM(walk_values.shape, bf16),
            pltpu.VMEM((nodes.shape[1], 3 * BS), bf16),
            pltpu.VMEM((2, *bias_query.shape), bf16),
            pltpu.VMEM(w_out.shape, bf16),
            pltpu.VMEM((wide * n_feat, rows // n_feat, nodes.shape[1]), bf16),
            pltpu.VMEM((wide * half, BS, BS), bf16),
            pltpu.VMEM((wide * half, BS, BS), bf16),
            pltpu.VMEM((wide * 2 * blocks, BS, BS), bf16),
            pltpu.VMEM((wide * blocks, BS, BS), bf16),
            pltpu.VMEM((n_feat * half, BS, BS), bf16),
            pltpu.VMEM((n_feat * half, BS, BS), bf16),
            pltpu.VMEM((n_feat, 2, 2, HD, BS), bf16),
            pltpu.VMEM((n_feat, 2, 2 * BS, 2 * BS), bf16),
            pltpu.VMEM((blocks, BS, BS), bf16),
            pltpu.VMEM((blocks, BS, BS), bf16),
            pltpu.VMEM((blocks * n_feat, BS, BS), bf16),
            pltpu.VMEM((blocks * (n_feat - 1), BS, BS), bf16),
            dma((2 * R,)),
            dma((2 * R,)),
            dma((2 * R,)),
            dma((2 * R,)),
            dma(()),
            dma(()),
            dma((2 * R,)),
            dma((2 * R,)),
            dma((n_feat - 1,)),
            dma((n_feat - 1,)),
            dma((n_feat - 1,)),
            dma((n_feat - 1,)),
            dma((2, n_feat - 1)),
            dma((2, n_feat - 1)),
            dma((blocks, n_feat - 1)),
            dma((blocks, n_feat - 1)),
            dma((2 * R,)),
            dma((2 * R,)),
            dma((2 * R,)),
            dma((2 * R,)),
            dma((2 * R,)),
            dma((2 * R,)),
            dma((2 * R,)),
            dma((2 * R,)),
            dma((13,)),
        ],
        compiler_params=pltpu.CompilerParams(
            collective_id=0, has_side_effects=True, vmem_limit_bytes=63 * 1024 * 1024
        ),
    )(
        walk_cols,
        walk_count,
        attn_cols,
        attn_count,
        nodes.reshape(n_feat, rows // n_feat, nodes.shape[1]),
        walk_state.T,
        walk_values,
        w_query,
        w_key,
        w_value,
        bias_query,
        bias_key,
        w_out,
    )
    return out, next_columns.T


def solution(mesh):
    placed = (
        P("dom", None),
        P("dom", "feat"),
        P("dom", None, None, None),
        P("dom", None),
        P("dom"),
        P("dom", None),
        P("dom"),
        P(None, "feat"),
        P(None, "feat"),
        P(None, "feat"),
        P(None, "feat", None),
        P(None, "feat", None),
        P("feat", None),
    )
    return jax.shard_map(
        on_device,
        mesh=mesh,
        in_specs=placed,
        out_specs=(P("dom", "feat"), P("dom", "feat")),
        check_vma=False,
    )
```
